32 devices in a mesh: dp: 8 (over y, x, core), mp: 4 (over z).
Axes of the slice: x: 2, y: 2, z: 4, core: 2. Of those that a mesh axis runs over, the one named last changes fastest.
Arguments:
- inputs: bfloat16 [16384, 768], P(('dp', 'mp')), may hold values from -6 to 6
- first_values: bfloat16 [16384, 384], P('dp'), may hold values from -6 to 6
- seq_lens: int32 [8], P('dp'), may hold values from 64 to 2048, as said below
- attn_gain: float32 [768], replicated, may hold values from 0.1 to 1.9
- attn_shift: float32 [768], replicated, may hold values from -3 to 3
- query_weight: bfloat16 [768, 768], P(None, 'mp'), may hold values from -0.21875 to 0.21875
- query_bias: float32 [768], P('mp'), may hold values from -3 to 3
- key_weight: bfloat16 [768, 768], P(None, 'mp'), may hold values from -0.21875 to 0.21875
- value_weight: bfloat16 [768, 384], replicated, may hold values from -0.21875 to 0.21875
- value_bias: float32 [384], replicated, may hold values from -3 to 3
- out_weight: bfloat16 [768, 768], P('mp'), may hold values from -0.875 to 0.875
- out_bias: float32 [768], replicated, may hold values from -3 to 3
- mlp_gain: float32 [768], replicated, may hold values from 0.1 to 1.9
- mlp_shift: float32 [768], replicated, may hold values from -3 to 3
- expand_weight: bfloat16 [768, 3072], P(None, 'mp'), may hold values from -0.21875 to 0.21875
- expand_bias: float32 [3072], P('mp'), may hold values from -3 to 3
- contract_weight: bfloat16 [3072, 768], P('mp'), may hold values from -0.109375 to 0.109375
- contract_bias: float32 [768], replicated, may hold values from -3 to 3
- cotangent: bfloat16 [16384, 768], P('dp'), may hold values from -6 to 6
Outputs:
- layer_out: bfloat16 [16384, 768], P(('dp', 'mp'))
- grad_inputs: float32 [16384, 768], P(('dp', 'mp'))
- grad_first_values: float32 [16384, 384], P('dp', 'mp')
- grad_attn_gain: float32 [768], replicated
- grad_attn_shift: float32 [768], replicated
- grad_query_weight: float32 [768, 768], P(None, 'mp')
- grad_query_bias: float32 [768], P('mp')
- grad_key_weight: float32 [768, 768], P(None, 'mp')
- grad_value_weight: float32 [768, 384], replicated
- grad_value_bias: float32 [384], replicated
- grad_out_weight: float32 [768, 768], P('mp')
- grad_out_bias: float32 [768], replicated
- grad_mlp_gain: float32 [768], replicated
- grad_mlp_shift: float32 [768], replicated
- grad_expand_weight: float32 [768, 3072], P(None, 'mp')
- grad_expand_bias: float32 [3072], P('mp')
- grad_contract_weight: float32 [3072, 768], P('mp')
- grad_contract_bias: float32 [768], replicated
The draws below stay inside these ranges and needn't reach their ends.
Inputs may be any that keep to these rules, and one draw needn't show every extreme that they name: `seq_lens`: each slot holds one sequence of that many positions followed by padding; in every draw one length is exactly 2048 and one is exactly 64.
All inputs are finite; a program needn't handle non-finite values.
Results may differ from the reference program's by a relative error of at most 0.015.
Values may be sent and summed in bfloat16 or wider, within the bound.
No kernel may reach another device: no remote copies, remote signals or barrier semaphores. Data moves between devices by JAX's collectives and lax.ppermute only.
A program may use at most 128 MiB of HBM per device.

```python
import jax
import jax.numpy as jnp
from jax import lax

D = 768
HEADS = 12
HEAD_DIM = 64
FF = 3072
SLOT_LEN = 2048
MIN_LEN = 64
SEQS = 8
TOKENS = 16384


def draw_seq_lens(key, part):
    key = jax.random.fold_in(key, 17)
    key_list = jax.random.split(key, 4)
    spread_len = SLOT_LEN - MIN_LEN
    first_draw = jax.random.randint(key_list[0], (SEQS,), 0, spread_len + 1)
    second_draw = jax.random.randint(key_list[1], (SEQS,), 0, spread_len + 1)
    lengths = SLOT_LEN - first_draw * second_draw // max(spread_len, 1)
    longest = jax.random.randint(key_list[2], (), 0, SEQS)
    shortest = (longest + 1 + jax.random.randint(key_list[3], (), 0, SEQS - 1)) % SEQS
    places = jnp.arange(SEQS, dtype=jnp.int32)
    lengths = jnp.where(places == longest, SLOT_LEN, lengths)
    lengths = jnp.where(places == shortest, MIN_LEN, lengths)
    return lengths.astype(jnp.int32)


def level_of(key, extent, shards, smallest, largest):
    factor_of, own = 1.0, jax.random.fold_in(key, 6)
    for position, shards_of in shards:
        steps = jnp.exp(jax.random.uniform(jax.random.fold_in(own, position), (shards_of,), jnp.float32, smallest / len(shards), largest / len(shards)))
        factor_of = factor_of * jnp.repeat(steps, extent[position] // shards_of).reshape([-1 if axis == position else 1 for axis in range(len(extent))])
    return factor_of


def normal_values(stream_key, dims, width, limit, cuts=(), held_as=jnp.bfloat16):
    factor_of = level_of(stream_key, dims, cuts, -0.22, 0.18) if cuts else 1.0
    array = jax.random.normal(stream_key, dims, jnp.float32) * width * factor_of
    return jnp.minimum(jnp.maximum(array, -limit), limit).astype(held_as)


def setup_inputs(seed: int = 0) -> dict:
    splits = jax.random.split(jax.random.key(seed), 20)
    inputs = normal_values(splits[0], (TOKENS, D), 1.0, 6.0, ((0, 32),))
    first_values = normal_values(splits[1], (TOKENS, D // 2), 1.0, 6.0, ((0, 8),))
    seq_lens = draw_seq_lens(jax.random.fold_in(splits[19], 71), 0)
    attn_gain = jnp.clip(1.0 + 0.18 * jax.random.normal(splits[3], (D,), jnp.float32), 0.1, 1.9)
    attn_shift = normal_values(splits[4], (D,), 0.5, 3.0, (), jnp.float32)
    query_weight = normal_values(splits[5], (D, D), D ** -0.5, 0.21875, ((1, 4),))
    query_bias = normal_values(splits[6], (D,), 0.5, 3.0, ((0, 4),), jnp.float32)
    key_weight = normal_values(splits[7], (D, D), D ** -0.5, 0.21875, ((1, 4),))
    value_weight = normal_values(splits[8], (D, D // 2), D ** -0.5, 0.21875)
    value_bias = normal_values(splits[9], (D // 2,), 0.5, 3.0, (), jnp.float32)
    out_weight = normal_values(splits[10], (D, D), (D // 16) ** -0.5, 0.875, ((0, 4),))
    out_bias = normal_values(splits[11], (D,), 0.5, 3.0, (), jnp.float32)
    mlp_gain = jnp.clip(1.0 + 0.18 * jax.random.normal(splits[12], (D,), jnp.float32), 0.1, 1.9)
    mlp_shift = normal_values(splits[13], (D,), 0.5, 3.0, (), jnp.float32)
    expand_weight = normal_values(splits[14], (D, FF), D ** -0.5, 0.21875, ((1, 4),))
    expand_bias = normal_values(splits[15], (FF,), 0.5, 3.0, ((0, 4),), jnp.float32)
    contract_weight = normal_values(splits[16], (FF, D), FF ** -0.5, 0.109375, ((0, 4),))
    contract_bias = normal_values(splits[17], (D,), 0.5, 3.0, (), jnp.float32)
    cotangent = normal_values(splits[18], (TOKENS, D), 1.0, 6.0, ((0, 8),))
    return dict(inputs=inputs, first_values=first_values, seq_lens=seq_lens, attn_gain=attn_gain, attn_shift=attn_shift, query_weight=query_weight, query_bias=query_bias, key_weight=key_weight, value_weight=value_weight, value_bias=value_bias, out_weight=out_weight, out_bias=out_bias, mlp_gain=mlp_gain, mlp_shift=mlp_shift, expand_weight=expand_weight, expand_bias=expand_bias, contract_weight=contract_weight, contract_bias=contract_bias, cotangent=cotangent)


@jax.custom_vjp
def low(v):
    return lax.optimization_barrier(v.astype(jnp.bfloat16)).astype(jnp.float32)

@jax.custom_vjp
def low_back(v):
    return v

def low_keep(v):
    return (low(v), None)

def low_pass(kept, grad):
    return (grad,)

def back_keep(v):
    return (v, None)

def back_low(kept, grad):
    return (low(grad),)
low.defvjp(low_keep, low_pass)
low_back.defvjp(back_keep, back_low)
NORM_EPS = 1e-05
MASKED = -1e+30

def layer_norm(values_in, gain, shift):
    centre = lax.optimization_barrier(jnp.mean(values_in, axis=-1, keepdims=True))
    centred = values_in - centre
    spread = lax.optimization_barrier(jnp.mean(centred * centred, axis=-1, keepdims=True))
    return centred * lax.rsqrt(spread + NORM_EPS) * gain + shift

def product(left, right):
    return jnp.dot(left, right, precision=lax.Precision.HIGHEST)

def slot_attention(pieces):
    queries, key_rows, value_rows, length = pieces
    query_heads = queries.reshape(SLOT_LEN, HEADS, HEAD_DIM)
    key_heads = key_rows.reshape(SLOT_LEN, HEADS, HEAD_DIM)
    value_heads = value_rows.reshape(SLOT_LEN, HEADS, HEAD_DIM)
    scores = jnp.einsum('qhd,khd->hqk', query_heads, key_heads, precision=lax.Precision.HIGHEST) * HEAD_DIM ** (-0.5)
    scores = low_back(scores)
    positions = jnp.arange(SLOT_LEN, dtype=jnp.int32)
    allowed = (positions[None, :] <= positions[:, None]) & (positions[None, :] < length)
    scores = jnp.where(allowed[None], scores, MASKED)
    probabilities = low(jax.nn.softmax(scores, axis=-1))
    mixture = jnp.einsum('hqk,khd->qhd', probabilities, value_heads, precision=lax.Precision.HIGHEST)
    return mixture.reshape(SLOT_LEN, HEADS * HEAD_DIM)

def reference(inputs, first_values, seq_lens, attn_gain, attn_shift, query_weight, query_bias, key_weight, value_weight, value_bias, out_weight, out_bias, mlp_gain, mlp_shift, expand_weight, expand_bias, contract_weight, contract_bias, cotangent):
    lengths = seq_lens.astype(jnp.int32)
    positions = jnp.arange(SLOT_LEN, dtype=jnp.int32)
    valid = (positions[None, :] < lengths[:, None]).reshape(-1)

    def to_slots(array_in):
        return array_in.reshape(SEQS, SLOT_LEN, HEADS * HEAD_DIM)

    def forward(residual, reused, gain_one, shift_one, w_query, b_query, w_key, w_value, b_value, w_out, b_out, gain_two, shift_two, w_expand, b_expand, w_contract, b_contract):
        normed_one = low(layer_norm(residual, gain_one, shift_one))
        queries = low_back(low(product(normed_one, w_query) + b_query))
        key_rows = low_back(low(product(normed_one, w_key)))
        value_rows = low_back(low(jnp.concatenate([product(normed_one, w_value) + b_value, reused], axis=1)))
        mixture = lax.map(jax.checkpoint(slot_attention), (to_slots(queries), to_slots(key_rows), to_slots(value_rows), lengths))
        heads_out = low_back(low(mixture.reshape(SEQS * SLOT_LEN, HEADS * HEAD_DIM)))
        attention = low_back(product(heads_out, w_out) + b_out)
        residual_two = residual + attention
        normed_two = low(layer_norm(residual_two, gain_two, shift_two))
        pre_act = low_back(product(normed_two, w_expand) + b_expand)
        hidden = low(jax.nn.gelu(pre_act))
        return residual_two + product(hidden, w_contract) + b_contract
    floats = [array_in.astype(jnp.float32) for array_in in (inputs, first_values, attn_gain, attn_shift, query_weight, query_bias, key_weight, value_weight, value_bias, out_weight, out_bias, mlp_gain, mlp_shift, expand_weight, expand_bias, contract_weight, contract_bias)]
    layer_value, backward = jax.vjp(forward, *floats)
    grad_out = jnp.where(valid[:, None], cotangent.astype(jnp.float32), jnp.zeros((), jnp.float32))
    grads = backward(grad_out)
    return (layer_value.astype(jnp.bfloat16), grads[0], grads[1], grads[2], grads[3], grads[4], grads[5], grads[6], grads[7], grads[8], grads[9], grads[10], grads[11], grads[12], grads[13], grads[14], grads[15], grads[16])
```

```python
import functools
import math

import jax
import jax.numpy as jnp
from jax import lax
from jax.experimental import pallas as pl
from jax.experimental.pallas import tpu as pltpu
from jax.sharding import PartitionSpec as P

HEAD_DIM = 64
TILE = 512
K_TILE = 256
NORM_EPS = 1e-05
MASKED = -1e30
EMPTY = 1e30
LOG2_E = 1.4426950408889634
SCALE = HEAD_DIM ** (-0.5)
BF16 = jnp.bfloat16
F32 = jnp.float32
CHUNKS = ((0, 1, 2),)


def dot(left, right, left_dim, right_dim):
    return lax.dot_general(
        left, right, (((left_dim,), (right_dim,)), ((), ())), preferred_element_type=F32
    )


def two_parts(value):
    high = value.astype(BF16)
    return high, (value - high.astype(F32)).astype(BF16)


def three_rows(value, row):
    first = value.astype(BF16)
    rest = value - first.astype(F32)
    second = rest.astype(BF16)
    third = (rest - second.astype(F32)).astype(BF16)
    parts = [part.astype(F32) for part in (first, second, third)]
    empty = jnp.zeros(row.shape, F32)
    rows = jnp.where(row == 0, parts[0], jnp.where(row == 1, parts[1], jnp.where(row == 2, parts[2], empty)))
    return rows.astype(BF16)


def forward_kernel(length_ref, query_ref, key_ref, value_ref, out_ref, log_ref, keys, queries, values):
    slot = query_ref.shape[1]
    length = length_ref[0]
    row = lax.broadcasted_iota(jnp.int32, (16, slot), 0)
    position = lax.broadcasted_iota(jnp.int32, (16, slot), 1)
    first_row = jnp.where(row == 0, 1.0, 0.0).astype(BF16)
    padding = jnp.where((row == 0) & (position >= length), MASKED, 0.0).astype(BF16)
    high, low = two_parts(query_ref[...].astype(F32) * (SCALE * LOG2_E))
    queries[0:64] = high
    queries[64:128] = low
    queries[128:144] = first_row
    key_cols = key_ref[...]
    keys[...] = jnp.concatenate([key_cols, key_cols, padding], axis=0).T
    values[0:64] = value_ref[...]
    values[64:80] = first_row
    key_pos = lax.broadcasted_iota(jnp.int32, (TILE, TILE), 0)
    query_pos = lax.broadcasted_iota(jnp.int32, (TILE, TILE), 1)
    for block in range(slot // TILE):
        begin, end = block * TILE, (block + 1) * TILE
        scores = jnp.dot(keys[0:end, :], queries[:, begin:end], preferred_element_type=F32)
        corner = jnp.where(key_pos <= query_pos, scores[begin:], MASKED)
        top = jnp.max(corner, axis=0, keepdims=True)
        if block:
            top = jnp.maximum(top, jnp.max(scores[:begin], axis=0, keepdims=True))
        mixed = jnp.dot(
            values[:, begin:end], jnp.exp2(corner - top).astype(BF16), preferred_element_type=F32
        )
        if block:
            mixed = mixed + jnp.dot(
                values[:, 0:begin],
                jnp.exp2(scores[:begin] - top).astype(BF16),
                preferred_element_type=F32,
            )
        total = mixed[64:65]
        out_ref[:, begin:end] = (mixed[0:64] / total).astype(BF16)
        place = lax.broadcasted_iota(jnp.int32, (1, TILE), 1) + begin
        log_ref[:, begin:end] = jnp.where(place < length, top + jnp.log2(total), EMPTY)


def backward_kernel(
    query_ref, key_ref, value_ref, out_ref, grad_ref, log_ref,
    grad_query_ref, grad_key_ref, grad_value_ref,
    keys, queries, values, grads, query_rows, grad_rows, key_total, value_total,
):
    slot = query_ref.shape[1]
    row = lax.broadcasted_iota(jnp.int32, (16, slot), 0)
    ones = jnp.where(row < 3, 1.0, 0.0).astype(BF16)
    query_cols = query_ref[...]
    key_cols = key_ref[...]
    grad_cols = grad_ref[...]
    high, low = two_parts(query_cols.astype(F32) * (SCALE * LOG2_E))
    queries[0:64] = high
    queries[64:128] = low
    queries[128:144] = three_rows(-log_ref[...], row)
    keys[...] = jnp.concatenate([key_cols, key_cols, ones], axis=0).T
    values[...] = jnp.concatenate([value_ref[...], ones], axis=0).T
    centre = jnp.sum(grad_cols.astype(F32) * out_ref[...].astype(F32), axis=0, keepdims=True)
    grads[0:64] = grad_cols
    grads[64:80] = three_rows(-centre, row)
    query_rows[...] = query_cols.T
    grad_rows[...] = grad_cols.T
    key_total[...] = jnp.zeros_like(key_total)
    value_total[...] = jnp.zeros_like(value_total)
    for block in range(slot // TILE):
        begin, end = block * TILE, (block + 1) * TILE
        grad_query = jnp.zeros((HEAD_DIM, TILE), F32)
        for start in range(0, end, K_TILE):
            span = slice(start, start + K_TILE)
            scores = jnp.dot(keys[span, :], queries[:, begin:end], preferred_element_type=F32)
            shifted = jnp.dot(values[span, :], grads[:, begin:end], preferred_element_type=F32)
            weights = jnp.exp2(scores)
            if start >= begin:
                key_pos = lax.broadcasted_iota(jnp.int32, (K_TILE, TILE), 0) + start
                query_pos = lax.broadcasted_iota(jnp.int32, (K_TILE, TILE), 1) + begin
                weights = jnp.where(key_pos <= query_pos, weights, 0.0)
            grad_scores = (weights * shifted).astype(BF16)
            value_total[span, :] += jnp.dot(
                weights.astype(BF16), grad_rows[begin:end, :], preferred_element_type=F32
            )
            key_total[span, :] += jnp.dot(
                grad_scores, query_rows[begin:end, :], preferred_element_type=F32
            )
            grad_query = grad_query + jnp.dot(
                key_cols[:, span], grad_scores, preferred_element_type=F32
            )
        grad_query_ref[:, begin:end] = (grad_query * SCALE).astype(BF16)
    grad_key_ref[...] = (key_total[...].T * SCALE).astype(BF16)
    grad_value_ref[...] = value_total[...].T.astype(BF16)


VMEM_BYTES = 48 * 1024 * 1024


def attend_forward(queries, key_rows, value_rows, seq_lens, heads):
    slot = queries.shape[1]
    count, first = len(heads), heads[0]
    spec = pl.BlockSpec((HEAD_DIM, slot), lambda h: (h + first, 0))
    return pl.pallas_call(
        forward_kernel,
        grid=(count,),
        in_specs=[pl.BlockSpec(memory_space=pltpu.SMEM), spec, spec, spec],
        out_specs=[
            pl.BlockSpec((HEAD_DIM, slot), lambda h: (h, 0)),
            pl.BlockSpec((None, 1, slot), lambda h: (h, 0, 0)),
        ],
        out_shape=[
            jax.ShapeDtypeStruct((count * HEAD_DIM, slot), BF16),
            jax.ShapeDtypeStruct((count, 1, slot), F32),
        ],
        scratch_shapes=[
            pltpu.VMEM((slot, 144), BF16),
            pltpu.VMEM((144, slot), BF16),
            pltpu.VMEM((80, slot), BF16),
        ],
        compiler_params=pltpu.CompilerParams(vmem_limit_bytes=VMEM_BYTES),
        cost_estimate=pl.CostEstimate(
            flops=count * 8 * slot * slot * HEAD_DIM,
            bytes_accessed=count * slot * HEAD_DIM * 8,
            transcendentals=count * slot * slot // 2,
        ),
        name="attend_forward",
    )(seq_lens, queries, key_rows, value_rows)


def attend_backward(queries, key_rows, value_rows, outputs, grads, logs, heads):
    slot = queries.shape[1]
    count, first = len(heads), heads[0]
    whole = pl.BlockSpec((HEAD_DIM, slot), lambda h: (h + first, 0))
    part = pl.BlockSpec((HEAD_DIM, slot), lambda h: (h, 0))
    log_spec = pl.BlockSpec((None, 1, slot), lambda h: (h, 0, 0))
    return pl.pallas_call(
        backward_kernel,
        grid=(count,),
        in_specs=[whole, whole, whole, part, part, log_spec],
        out_specs=[part, part, part],
        out_shape=[jax.ShapeDtypeStruct((count * HEAD_DIM, slot), BF16)] * 3,
        scratch_shapes=[
            pltpu.VMEM((slot, 144), BF16),
            pltpu.VMEM((144, slot), BF16),
            pltpu.VMEM((slot, 80), BF16),
            pltpu.VMEM((80, slot), BF16),
            pltpu.VMEM((slot, HEAD_DIM), BF16),
            pltpu.VMEM((slot, HEAD_DIM), BF16),
            pltpu.VMEM((slot, HEAD_DIM), F32),
            pltpu.VMEM((slot, HEAD_DIM), F32),
        ],
        compiler_params=pltpu.CompilerParams(vmem_limit_bytes=VMEM_BYTES),
        cost_estimate=pl.CostEstimate(
            flops=count * 20 * slot * slot * HEAD_DIM,
            bytes_accessed=count * slot * HEAD_DIM * 16,
            transcendentals=count * slot * slot // 2,
        ),
        name="attend_backward",
    )(queries, key_rows, value_rows, outputs, grads, logs)


def normalize(values_in):
    centre = jnp.mean(values_in, axis=-1, keepdims=True)
    centred = values_in - centre
    spread = jnp.mean(centred * centred, axis=-1, keepdims=True)
    inverse = lax.rsqrt(spread + NORM_EPS)
    return centred * inverse, inverse


def normalize_back(normed, inverse, grads, gain):
    scaled = grads * gain
    mean_scaled = jnp.mean(scaled, axis=-1, keepdims=True)
    mean_product = jnp.mean(scaled * normed, axis=-1, keepdims=True)
    return inverse * (scaled - mean_scaled - normed * mean_product)


def gelu_parts(value):
    root = math.sqrt(2.0 / math.pi)
    bent = jnp.tanh(root * (value + 0.044715 * value * value * value))
    out = 0.5 * value * (1.0 + bent)
    slope = 0.5 * (1.0 + bent) + 0.5 * value * (1.0 - bent * bent) * root * (
        1.0 + 3 * 0.044715 * value * value
    )
    return out, slope


def line_gather(block, axis, size, member):
    rows = block.shape[0]
    up = down = block
    ups, downs = [], []
    for _ in range(size - 1):
        up = lax.ppermute(up, axis, [(i, i + 1) for i in range(size - 1)])
        down = lax.ppermute(down, axis, [(i + 1, i) for i in range(size - 1)])
        ups.append(up)
        downs.append(down)
    ordered = jnp.concatenate(ups[::-1] + [block] + downs, axis=0)
    return lax.dynamic_slice_in_dim(ordered, (size - 1 - member) * rows, size * rows, 0)


def exchange(pieces, axis):
    return lax.all_to_all(pieces, axis, 0, 0)


def cube_bits(size):
    return [1 << bit for bit in range(size.bit_length() - 1)]


def cube_sum(value, axis, size):
    for bit in cube_bits(size):
        value = value + lax.ppermute(value, axis, [(i, i ^ bit) for i in range(size)])
    return value


def shift_sum(value, axis, size):
    total = value
    for shift in range(1, size):
        total = total + lax.ppermute(value, axis, [(i, (i + shift) % size) for i in range(size)])
    return total


def cube_scatter(value, axis, size, index):
    for bit in cube_bits(size)[::-1]:
        halves = value.reshape((2, value.shape[0] // 2) + value.shape[1:])
        side = (index // bit) % 2
        kept = lax.dynamic_index_in_dim(halves, side, 0, keepdims=False)
        given = lax.dynamic_index_in_dim(halves, 1 - side, 0, keepdims=False).astype(BF16)
        came = lax.ppermute(given, axis, [(i, i ^ bit) for i in range(size)])
        value = kept + came.astype(F32)
    return value


def cube_gather(value, axis, size, index):
    for bit in cube_bits(size):
        came = lax.ppermute(value, axis, [(i, i ^ bit) for i in range(size)])
        side = (index // bit) % 2
        value = jnp.where(
            side == 1, jnp.concatenate([came, value], 0), jnp.concatenate([value, came], 0)
        )
    return value


def shards(
    mp_size, dp_size,
    inputs, first_values, seq_lens, attn_gain, attn_shift, query_weight, query_bias, key_weight,
    value_weight, value_bias, out_weight, out_bias, mlp_gain, mlp_shift, expand_weight, expand_bias,
    contract_weight, contract_bias, cotangent,
):
    member = lax.axis_index("mp")
    group = lax.axis_index("dp")
    share_rows, width = inputs.shape
    slot = share_rows * mp_size
    head_cols = query_weight.shape[1]
    fresh_count = mp_size // 2
    fresh = member < fresh_count
    value_start = member % fresh_count * head_cols
    half_width = value_weight.shape[1]

    def gather_weight(shards_of):
        pieces = []
        for shard in shards_of:
            rows = shard.shape[0] // dp_size
            pieces.append(lax.dynamic_slice_in_dim(shard, group * rows, rows, 0))
        whole = lax.all_gather(jnp.concatenate(pieces), ("mp", "dp"), axis=0, tiled=False)
        parts, begin = [], 0
        for piece in pieces:
            rows = piece.shape[0]
            parts.append(whole[:, begin : begin + rows].reshape(-1, width))
            begin += rows
        return parts

    residual = inputs.astype(F32)
    plain_one, inverse_one = normalize(residual)
    normed_one = (plain_one * attn_gain + attn_shift).astype(BF16)
    bias_rows = three_rows(jnp.broadcast_to(expand_bias, (16, expand_bias.shape[0])), lax.broadcasted_iota(jnp.int32, (16, width), 0))
    gathered = line_gather(jnp.concatenate([normed_one, bias_rows]), "mp", mp_size, member)
    gathered = gathered.reshape(mp_size, share_rows + 16, width)
    full_one = gathered[:, :share_rows].reshape(slot, width)
    expand_shift = jnp.sum(gathered[:, share_rows : share_rows + 3].astype(F32), axis=1).reshape(-1)
    out_all, expand_all = gather_weight((out_weight, expand_weight.T))
    (contract_all,) = gather_weight((contract_weight,))
    query_all, key_all = gather_weight((query_weight.T, key_weight.T))

    value_cols = lax.dynamic_slice_in_dim(value_weight, value_start, head_cols, 1)
    value_offset = lax.dynamic_slice_in_dim(value_bias, value_start, head_cols, 0)
    reused = lax.dynamic_slice_in_dim(first_values, value_start, head_cols, 1).T
    joined = jnp.concatenate([query_weight, key_weight, value_cols], axis=1)
    offsets = jnp.concatenate([query_bias, jnp.zeros_like(query_bias), value_offset])
    projected = (dot(joined, full_one, 0, 1) + offsets[:, None]).astype(BF16)
    queries = projected[:head_cols]
    key_rows = projected[head_cols : 2 * head_cols]
    value_rows = jnp.where(fresh, projected[2 * head_cols :], reused)

    logs, outputs, arrived = [], [], []
    for heads in CHUNKS:
        out, log = attend_forward(queries, key_rows, value_rows, seq_lens, heads)
        outputs.append(out)
        logs.append(log)
        pieces = out.reshape(out.shape[0], mp_size, share_rows).transpose(1, 0, 2)
        arrived.append(exchange(pieces, "mp"))
    heads_out = jnp.concatenate(arrived, axis=1).reshape(width, share_rows)

    residual_two = residual + dot(heads_out, out_all, 0, 0) + out_bias
    plain_two, inverse_two = normalize(residual_two)
    normed_two = (plain_two * mlp_gain + mlp_shift).astype(BF16)
    pre_act = dot(normed_two, expand_all, 1, 1) + expand_shift
    hidden, slope = gelu_parts(pre_act)
    hidden = hidden.astype(BF16)
    layer_out = (residual_two + dot(hidden, contract_all, 1, 0) + contract_bias).astype(BF16)

    places = member * share_rows + jnp.arange(share_rows, dtype=jnp.int32)
    own_cotangent = lax.dynamic_slice_in_dim(cotangent, member * share_rows, share_rows, 0)
    grad_out = jnp.where((places < seq_lens[0])[:, None], own_cotangent, jnp.zeros_like(own_cotangent))
    grad_pre = (dot(grad_out, contract_all, 1, 1) * slope).astype(BF16)

    def sum_weight(grad):
        rows = grad.shape[0] // (mp_size * dp_size)
        pieces = grad.astype(BF16).reshape(mp_size, dp_size, rows, width)
        pieces = lax.psum_scatter(pieces, "dp", scatter_dimension=1, tiled=False)
        piece = lax.psum_scatter(pieces, "mp", scatter_dimension=0, tiled=False)
        return lax.all_gather(piece, "dp", axis=0, tiled=True).astype(F32)

    grad_contract = sum_weight(dot(hidden, grad_out, 0, 0))
    grad_expand = sum_weight(dot(grad_pre, normed_two, 0, 0)).T
    grad_normed_two = dot(grad_pre, expand_all, 1, 0)
    grad_resid_two = grad_out.astype(F32) + normalize_back(plain_two, inverse_two, grad_normed_two, mlp_gain)
    grad_attn = grad_resid_two.astype(BF16)
    grad_out_weight = sum_weight(dot(heads_out, grad_attn, 1, 0))
    early = jnp.concatenate(
        [
            jnp.sum(grad_normed_two * plain_two, axis=0),
            jnp.sum(grad_normed_two, axis=0),
            jnp.sum(grad_attn.astype(F32), axis=0),
            jnp.sum(grad_out.astype(F32), axis=0),
            jnp.sum(grad_pre.astype(F32), axis=0),
        ]
    ).reshape(-1, width)
    early = shift_sum(cube_sum(early, "dp", dp_size), "mp", mp_size)

    grad_heads = dot(out_all, grad_attn, 1, 1).astype(BF16).reshape(mp_size, head_cols, share_rows)
    grads_back = []
    for heads, out, log in zip(CHUNKS, outputs, logs):
        rows = slice(heads[0] * HEAD_DIM, (heads[-1] + 1) * HEAD_DIM)
        came = exchange(grad_heads[:, rows], "mp")
        grad_full = came.transpose(1, 0, 2).reshape(-1, slot)
        grads_back.append(attend_backward(queries, key_rows, value_rows, out, grad_full, log, heads))

    returned = []
    for grads in grads_back:
        packed = jnp.stack([grads[0], grads[1], jnp.where(fresh, grads[2], jnp.zeros_like(grads[2]))])
        pieces = packed.reshape(3, -1, mp_size, share_rows).transpose(2, 0, 1, 3)
        returned.append(exchange(pieces, "mp"))
    grad_queries, grad_keys, grad_values = [
        jnp.concatenate([part[index] for part in grads_back], axis=0)
        for index in range(3)
    ]
    own = jnp.concatenate(returned, axis=2)
    own_queries = own[:, 0].reshape(width, share_rows)
    own_keys = own[:, 1].reshape(width, share_rows)
    own_values = own[:fresh_count, 2].reshape(half_width, share_rows)
    grad_normed_one = (
        dot(own_queries, query_all, 0, 0) + dot(own_keys, key_all, 0, 0) + dot(own_values, value_weight, 0, 1)
    )
    grad_inputs = grad_resid_two + normalize_back(plain_one, inverse_one, grad_normed_one, attn_gain)

    grad_joined = dot(jnp.concatenate([grad_queries, grad_keys, grad_values]), full_one, 1, 0)
    piece = cube_scatter(grad_joined.T, "dp", dp_size, group)
    own_value = piece[:, 2 * head_cols :] * jnp.where(fresh, 1.0, 0.0)
    value_piece = lax.dynamic_update_slice_in_dim(
        jnp.zeros((piece.shape[0], half_width), F32), own_value, value_start, 1
    )
    value_piece = shift_sum(value_piece.astype(BF16), "mp", mp_size)
    whole = cube_gather(
        jnp.concatenate([piece[:, : 2 * head_cols].astype(BF16), value_piece], axis=1), "dp", dp_size, group
    ).astype(F32)
    grad_query_weight = whole[:, :head_cols]
    grad_key_weight = whole[:, head_cols : 2 * head_cols]
    grad_value_weight = whole[:, 2 * head_cols :]

    out_cols = half_width // mp_size
    halves = grad_values.reshape(2, out_cols, slot)
    first_parts = [
        lax.ppermute(
            halves[part], "mp", [(fresh_count + i, 2 * i + part) for i in range(mp_size - fresh_count)]
        )
        for part in range(2)
    ]
    grad_first_values = jnp.where(member % 2 == 0, first_parts[0], first_parts[1]).astype(F32).T

    fresh_scale = jnp.where(fresh, 1.0, 0.0)
    query_sums = jnp.sum(grad_queries.astype(F32), axis=1)
    value_sums = jnp.sum(grad_values.astype(F32), axis=1) * fresh_scale
    late = jnp.concatenate(
        [
            jnp.sum(grad_normed_one * plain_one, axis=0),
            jnp.sum(grad_normed_one, axis=0),
            lax.dynamic_update_slice_in_dim(jnp.zeros((width,), F32), query_sums, member * head_cols, 0),
            lax.dynamic_update_slice_in_dim(jnp.zeros((width,), F32), value_sums, value_start, 0),
        ]
    ).reshape(-1, width)
    late = shift_sum(cube_sum(late, "dp", dp_size), "mp", mp_size)
    hidden_share = expand_bias.shape[0]
    return (
        layer_out,
        grad_inputs,
        grad_first_values,
        late[0],
        late[1],
        grad_query_weight,
        lax.dynamic_slice_in_dim(late[2], member * head_cols, head_cols, 0),
        grad_key_weight,
        grad_value_weight,
        late[3, :half_width],
        grad_out_weight,
        early[2],
        early[0],
        early[1],
        grad_expand,
        lax.dynamic_slice_in_dim(early[4:].reshape(-1), member * hidden_share, hidden_share, 0),
        grad_contract,
        early[3],
    )


def solution(mesh):
    rows, cols, both = P(("dp", "mp"), None), P(None, "mp"), P("mp", None)
    return jax.shard_map(
        functools.partial(shards, mesh.shape["mp"], mesh.shape["dp"]),
        mesh=mesh,
        in_specs=(
            rows, P("dp", None), P("dp"), P(), P(), cols, P("mp"), cols, P(), P(),
            both, P(), P(), P(), cols, P("mp"), both, P(), P("dp", None),
        ),
        out_specs=(
            rows, rows, P("dp", "mp"), P(), P(), cols, P("mp"), cols, P(), P(),
            both, P(), P(), P(), cols, P("mp"), both, P(),
        ),
        check_vma=False,
    )
```
